32 devices in a mesh: dp: 16 (over z, y, core), mp: 2 (over x).
Axes of the slice: x: 2, y: 2, z: 4, core: 2. Of those that a mesh axis runs over, the one named last changes fastest.
Arguments:
- tokens: bfloat16 [64, 512, 1024], P('dp'), may hold values from -6 to 6
- cotangent: bfloat16 [64, 512, 1024], P('dp', None, 'mp'), may hold values from -6 to 6
- segment_ids: int32 [64, 512], P('dp'), may hold values from 0 to 3, as said below
- positions: int32 [64, 512], P('dp'), may hold values from 0 to 1725, as said below
- attn_gain: bfloat16 [1024], replicated, may hold values from 0.099609375 to 1.8984375
- w_query: bfloat16 [1024, 1024], P('dp', 'mp'), may hold values from -0.1875 to 0.1875
- key_value_weight: bfloat16 [1024, 8, 128], P('dp', 'mp'), may hold values from -0.1875 to 0.1875
- w_out: bfloat16 [1024, 1024], P('mp', 'dp'), may hold values from -1.5 to 1.5
- qk_gain: bfloat16 [2, 64], replicated, may hold values from 0.099609375 to 1.8984375
- ffn_gain: bfloat16 [1024], replicated, may hold values from 0.099609375 to 1.8984375
- w_gateup: bfloat16 [1024, 2, 4608], P('dp', None, 'mp'), may hold values from -0.1875 to 0.1875
- w_down: bfloat16 [4608, 1024], P('mp', 'dp'), may hold values from -0.09375 to 0.09375
Outputs:
- mixed: bfloat16 [64, 512, 1024], P('dp', None, 'mp')
- tokens_grad: float32 [64, 512, 1024], P('dp', None, 'mp')
- attn_gain_grad: float32 [1024], replicated
- w_query_grad: float32 [1024, 1024], P('dp', 'mp')
- w_keyval_grad: float32 [1024, 8, 128], P('dp', 'mp')
- w_out_grad: float32 [1024, 1024], P('mp', 'dp')
- qk_gain_grad: float32 [2, 64], replicated
- ffn_gain_grad: float32 [1024], replicated
- w_gateup_grad: float32 [1024, 2, 4608], P('dp', None, 'mp')
- w_down_grad: float32 [4608, 1024], P('mp', 'dp')
The draws below stay inside these ranges and needn't reach their ends.
Inputs may be any that keep to these rules, and one draw needn't show every extreme that they name: `segment_ids`: each sequence holds four documents numbered 0 to 3 in order, each of one token or more. `positions`: positions rise by one within a document and start at 0, except that a sequence's first document may continue one begun before it, from an offset of at most 1535; the largest position is 1725.
All inputs are finite; a program needn't handle non-finite values.
Results may differ from the reference program's by a relative error of at most 0.017.
Values may be sent and summed in bfloat16 or wider, within the bound.
A program may use at most 256 MiB of HBM per device.

```python
import jax
import jax.numpy as jnp
from jax import lax

MODEL_WIDTH = 1024
QUERY_HEADS = 16
KEY_VALUE_HEADS = 8
HEAD_SIZE = 64
FF = 4608
SEQUENCE_TOKENS = 512
SEQ_DEV = 4
BATCH = 64
N_DP = 16


def document_layout(key):
    first, second, third, shift, chosen = jax.random.split(key, 5)
    order = jnp.arange(SEQUENCE_TOKENS, dtype=jnp.int32)[None, :]
    rows = jnp.arange(BATCH, dtype=jnp.int32)[:, None]
    picked = jax.random.randint(chosen, (), 0, BATCH)
    cut_one = jax.random.randint(first, (BATCH, 1), SEQUENCE_TOKENS // 8, 3 * SEQUENCE_TOKENS // 8)
    cut_one = jnp.where(rows == picked, 3 * SEQUENCE_TOKENS // 8 - 1, cut_one)
    cut_two = jax.random.randint(second, (BATCH, 1), 3 * SEQUENCE_TOKENS // 8, 5 * SEQUENCE_TOKENS // 8)
    cut_three = jax.random.randint(third, (BATCH, 1), 5 * SEQUENCE_TOKENS // 8, 7 * SEQUENCE_TOKENS // 8)
    segment = (order >= cut_one).astype(jnp.int32) + (order >= cut_two).astype(jnp.int32) + (order >= cut_three).astype(jnp.int32)
    begin = jnp.where(segment == 0, 0, jnp.where(segment == 1, cut_one, jnp.where(segment == 2, cut_two, cut_three)))
    offset = jax.random.randint(shift, (BATCH, 1), 0, 1536)
    offset = jnp.where(rows == picked, 1535, offset)
    position = order - begin + jnp.where(segment == 0, offset, 0)
    return (segment.astype(jnp.int32), position.astype(jnp.int32))


def draw_segment_ids(key, part):
    segment, position = document_layout(key)
    return segment


def draw_positions(key, part):
    segment, position = document_layout(key)
    return position


def levels(own_key, dims, cuts, least, largest):
    def one(dim, shards_of):
        steps = jax.random.uniform(jax.random.fold_in(jax.random.fold_in(own_key, 6), dim), (shards_of,), jnp.float32, least / len(cuts), largest / len(cuts))
        return jnp.repeat(jnp.exp(steps), dims[dim] // shards_of).reshape((-1,) + (1,) * (len(dims) - dim - 1))

    loudness = one(*cuts[0])
    for cut in cuts[1:]:
        loudness = loudness * one(*cut)
    return loudness


def scatter_about(stream_key, shape, spread, most, pieces=(), kind=jnp.bfloat16):
    array = jax.random.normal(stream_key, shape, jnp.float32) * spread
    if len(pieces) > 0:
        array = levels(stream_key, shape, pieces, -0.22, 0.18) * array
    return jnp.clip(array, min=-most, max=most).astype(kind)


def setup_inputs(seed: int = 0) -> dict:
    arg_keys = jax.random.split(jax.random.key(seed), 13)
    tokens = scatter_about(arg_keys[0], (BATCH, SEQUENCE_TOKENS, MODEL_WIDTH), 1.0, 6.0, ((0, 16),))
    cotangent = scatter_about(arg_keys[1], (BATCH, SEQUENCE_TOKENS, MODEL_WIDTH), 1.0, 6.0, ((0, 16), (2, 2)))
    segment_ids = draw_segment_ids(jax.random.fold_in(arg_keys[12], 71), 0)
    positions = draw_positions(jax.random.fold_in(arg_keys[12], 71), 0)
    attn_gain = jnp.clip(1.0 + 0.18 * jax.random.normal(arg_keys[4], (MODEL_WIDTH,), jnp.float32), 0.099609375, 1.8984375).astype(jnp.bfloat16)
    w_query = scatter_about(arg_keys[5], (MODEL_WIDTH, QUERY_HEADS * HEAD_SIZE), MODEL_WIDTH ** -0.5, 0.1875, ((0, 16), (1, 2)))
    key_value_weight = scatter_about(arg_keys[6], (MODEL_WIDTH, KEY_VALUE_HEADS, 2 * HEAD_SIZE), MODEL_WIDTH ** -0.5, 0.1875, ((0, 16), (1, 2)))
    w_out = scatter_about(arg_keys[7], (QUERY_HEADS * HEAD_SIZE, MODEL_WIDTH), (QUERY_HEADS * HEAD_SIZE // 64) ** -0.5, 1.5, ((0, 2), (1, 16)))
    qk_gain = jnp.clip(1.0 + 0.18 * jax.random.normal(arg_keys[8], (2, HEAD_SIZE), jnp.float32), 0.099609375, 1.8984375).astype(jnp.bfloat16)
    ffn_gain = jnp.clip(1.0 + 0.18 * jax.random.normal(arg_keys[9], (MODEL_WIDTH,), jnp.float32), 0.099609375, 1.8984375).astype(jnp.bfloat16)
    w_gateup = scatter_about(arg_keys[10], (MODEL_WIDTH, 2, FF), MODEL_WIDTH ** -0.5, 0.1875, ((0, 16), (2, 2)))
    w_down = scatter_about(arg_keys[11], (FF, MODEL_WIDTH), FF ** -0.5, 0.09375, ((0, 2), (1, 16)))
    return dict(tokens=tokens, cotangent=cotangent, segment_ids=segment_ids, positions=positions, attn_gain=attn_gain, w_query=w_query, key_value_weight=key_value_weight, w_out=w_out, qk_gain=qk_gain, ffn_gain=ffn_gain, w_gateup=w_gateup, w_down=w_down)


epsilon = 1e-05
rope_base = 1000000.0

@jax.custom_vjp
def low(v):
    return lax.optimization_barrier(v.astype(jnp.bfloat16)).astype(jnp.float32)

@jax.custom_vjp
def lower_backward(v):
    return v

def low_keep(v):
    return (low(v), None)

def low_pass(kept, grad):
    return (grad,)

def back_keep(v):
    return (v, None)

def back_low(kept, grad):
    return (low(grad),)
low.defvjp(low_keep, low_pass)
lower_backward.defvjp(back_keep, back_low)

def matrix_product(left, right):
    return jnp.dot(left, right, precision=lax.Precision.HIGHEST, preferred_element_type=jnp.float32)

def rms_scale(value, gain):
    return value * lax.rsqrt(lax.optimization_barrier(jnp.mean(value * value, axis=-1, keepdims=True)) + epsilon) * gain

def rotate(value, place):
    half = HEAD_SIZE // 2
    frequency = rope_base ** (-(jnp.arange(half, dtype=jnp.float32) * 2.0 / HEAD_SIZE))
    angle = place.astype(jnp.float32)[..., None] * frequency
    cosine = jnp.cos(angle)[..., None, :]
    sine = jnp.sin(angle)[..., None, :]
    first, second = (value[..., :half], value[..., half:])
    return jnp.concatenate([first * cosine - second * sine, second * cosine + first * sine], axis=-1)

def attend_one(item):
    query_rot, key_rot, values, segment = item
    shared_portion = QUERY_HEADS // KEY_VALUE_HEADS
    keys_all = jnp.repeat(key_rot, shared_portion, axis=1)
    values_all = jnp.repeat(values, shared_portion, axis=1)
    scores = jnp.einsum('qhd,khd->hqk', query_rot, keys_all, precision=lax.Precision.HIGHEST) * HEAD_SIZE ** (-0.5)
    order = jnp.arange(SEQUENCE_TOKENS)
    mask = (segment[:, None] == segment[None, :]) & (order[None, :] <= order[:, None])
    scores = lower_backward(jnp.where(mask[None], scores, -1e+30))
    top = lax.optimization_barrier(jnp.max(scores, axis=-1, keepdims=True))
    expo = jnp.exp(scores - top)
    probs = expo / lax.optimization_barrier(jnp.sum(expo, axis=-1, keepdims=True))
    attended = jnp.einsum('hqk,khd->qhd', low(probs), values_all, precision=lax.Precision.HIGHEST)
    return attended.reshape(SEQUENCE_TOKENS, QUERY_HEADS * HEAD_SIZE)

def layer(block, segment, place, gain_first, query_w, key_value_matrix, out_w, pair_gain, gain_second, gateup_w, down_w):
    token_count = block.shape[0]
    rows = token_count * SEQUENCE_TOKENS
    first_normed_input = low(rms_scale(block, gain_first)).reshape(rows, MODEL_WIDTH)
    query = lower_backward(matrix_product(first_normed_input, query_w)).reshape(token_count, SEQUENCE_TOKENS, QUERY_HEADS, HEAD_SIZE)
    key_value_rows = lower_backward(matrix_product(first_normed_input, key_value_matrix.reshape(MODEL_WIDTH, KEY_VALUE_HEADS * 2 * HEAD_SIZE))).reshape(token_count, SEQUENCE_TOKENS, KEY_VALUE_HEADS, 2 * HEAD_SIZE)
    query_rot = low(rotate(rms_scale(query, pair_gain[0]), place))
    key_rot = low(rotate(rms_scale(key_value_rows[..., :HEAD_SIZE], pair_gain[1]), place))
    values = low(key_value_rows[..., HEAD_SIZE:])
    attended = lax.map(jax.checkpoint(attend_one), (query_rot, key_rot, values, segment))
    attended = low(lower_backward(attended)).reshape(rows, QUERY_HEADS * HEAD_SIZE)
    resid = block + lower_backward(matrix_product(attended, out_w)).reshape(token_count, SEQUENCE_TOKENS, MODEL_WIDTH)
    normed_second = low(rms_scale(resid, gain_second)).reshape(rows, MODEL_WIDTH)
    gateup = matrix_product(normed_second, gateup_w.reshape(MODEL_WIDTH, 2 * FF))
    gate = lower_backward(gateup[:, :FF])
    upper = lower_backward(gateup[:, FF:])
    hidden = low(jax.nn.silu(gate) * upper)
    return resid + lower_backward(matrix_product(hidden, down_w)).reshape(token_count, SEQUENCE_TOKENS, MODEL_WIDTH)

def reference(tokens, cotangent, segment_ids, positions, attn_gain, w_query, key_value_weight, w_out, qk_gain, ffn_gain, w_gateup, w_down):
    params = tuple((value.astype(jnp.float32) for value in (attn_gain, w_query, key_value_weight, w_out, qk_gain, ffn_gain, w_gateup, w_down)))
    blocks = tokens.astype(jnp.float32).reshape(N_DP, SEQ_DEV, SEQUENCE_TOKENS, MODEL_WIDTH)
    grads = cotangent.astype(jnp.float32).reshape(N_DP, SEQ_DEV, SEQUENCE_TOKENS, MODEL_WIDTH)
    segments = segment_ids.reshape(N_DP, SEQ_DEV, SEQUENCE_TOKENS)
    places = positions.reshape(N_DP, SEQ_DEV, SEQUENCE_TOKENS)

    def group(totals, item):
        block, grad, segment, place = item

        def forward(value, *weights):
            return layer(value, segment, place, *weights)
        output, pullback = jax.vjp(forward, block, *params)
        pulled = pullback(grad)
        totals = tuple((total + term for total, term in zip(totals, pulled[1:])))
        return (totals, (output.astype(jnp.bfloat16), pulled[0]))
    start = tuple((jnp.zeros(value.shape, jnp.float32) for value in params))
    totals, (mixed, tokens_grad) = lax.scan(group, start, (blocks, grads, segments, places))
    return (mixed.reshape(BATCH, SEQUENCE_TOKENS, MODEL_WIDTH), tokens_grad.reshape(BATCH, SEQUENCE_TOKENS, MODEL_WIDTH), totals[0], totals[1], totals[2], totals[3], totals[4], totals[5], totals[6], totals[7])
```

```python
import jax
import jax.numpy as jnp
from jax import lax
from jax.sharding import PartitionSpec as P

HEAD_SIZE = 64
CHUNKS = 2

epsilon = 1e-05
rope_base = 1000000.0
f32 = jnp.float32
bf16 = jnp.bfloat16


def rotate_table(place):
    half = HEAD_SIZE // 2
    frequency = rope_base ** (-(jnp.arange(half, dtype=f32) * 2.0 / HEAD_SIZE))
    angle = place.astype(f32)[:, None] * frequency[None, :]
    return (jnp.cos(angle)[:, None, :], jnp.sin(angle)[:, None, :])


def rotate(value, cosine, sine):
    half = HEAD_SIZE // 2
    first, second = (value[..., :half], value[..., half:])
    return jnp.concatenate(
        [first * cosine - second * sine, second * cosine + first * sine], axis=-1
    )


def head_norm(value, gain):
    scale = lax.rsqrt(jnp.mean(value * value, axis=-1, keepdims=True) + epsilon)
    unit = value * scale
    return (unit * gain, unit, scale)


def head_norm_back(grad, unit, scale, gain):
    scaled = grad * gain
    inner = jnp.mean(unit * scaled, axis=-1, keepdims=True)
    return (scale * (scaled - unit * inner), jnp.sum(grad * unit, axis=(0, 1)))


def gather_rows(part):
    return lax.all_gather(part, "dp", axis=0, tiled=True)


def scatter_rows(total):
    return lax.psum_scatter(total, "dp", scatter_dimension=0, tiled=True).astype(f32)


def after(value, *earlier):
    return lax.optimization_barrier((value,) + earlier)


def shift(value, step):
    parts = lax.axis_size("mp")
    return lax.ppermute(value, "mp", [((i + step) % parts, i) for i in range(parts)])


def whole(own):
    parts = lax.axis_size("mp")
    index = lax.axis_index("mp")
    pieces = [own] + [shift(own, step) for step in range(1, parts)]
    placed = []
    for spot in range(parts):
        piece = pieces[spot]
        for holder in range(1, parts):
            piece = jnp.where(index == holder, pieces[(spot - holder) % parts], piece)
        placed.append(piece)
    return jnp.concatenate(placed, axis=1)


def row_sum(value):
    parts = lax.axis_size("mp")
    total = value
    for step in range(1, parts):
        total = total + shift(value, step)
    return total


def branch(value, rows):
    parts = lax.axis_size("mp")
    index = lax.axis_index("mp")
    width = rows.shape[0] // parts

    def term(owner, kind):
        piece = lax.dynamic_slice_in_dim(rows, owner * width, width, 0)
        return lax.dot_general(
            value, piece, (((1,), (1,)), ((), ())), preferred_element_type=f32
        ).astype(kind)

    got = []
    for step in range(1, parts):
        got.append(shift(term(lax.rem(index + parts - step, parts), bf16), step))
    total = term(index, f32)
    for piece in got:
        total = total + piece.astype(f32)
    return total


def over_tokens(left, right):
    left = jnp.concatenate(left, axis=0)
    right = jnp.concatenate(right, axis=0)
    return lax.dot_general(
        left, right, (((0,), (0,)), ((), ())), preferred_element_type=f32
    ).astype(bf16)


def score(query_rot, key_rot, segment):
    length, kv_heads = (key_rot.shape[0], key_rot.shape[1])
    order = jnp.arange(length)
    mask = (segment[:, None] == segment[None, :]) & (order[None, :] <= order[:, None])
    grouped = query_rot.reshape(length, kv_heads, -1, HEAD_SIZE)
    scores = jnp.einsum(
        "qhgd,khd->hgqk", grouped, key_rot, preferred_element_type=f32
    ) * HEAD_SIZE ** (-0.5)
    return jnp.where(mask, scores, -1e30)


def attend(scores, values):
    length = values.shape[0]
    top = jnp.max(scores, axis=-1, keepdims=True)
    expo = jnp.exp(scores - top)
    total = jnp.sum(expo, axis=-1, keepdims=True)
    weights = (expo / total).astype(bf16)
    attended = jnp.einsum("hgqk,khd->qhgd", weights, values, preferred_element_type=f32)
    return (attended.reshape(length, -1).astype(bf16), weights)


def attend_back(query_rot, key_rot, values, weights, attended, grad_out):
    length, kv_heads = (key_rot.shape[0], key_rot.shape[1])
    shape = (length, kv_heads, -1, HEAD_SIZE)
    grouped = query_rot.reshape(shape)
    grad_grouped = grad_out.reshape(shape)
    inner = jnp.sum(attended.reshape(shape).astype(f32) * grad_grouped.astype(f32), axis=-1)
    inner = inner.transpose(1, 2, 0)[..., None]
    grad_probs = jnp.einsum("qhgd,khd->hgqk", grad_grouped, values, preferred_element_type=f32)
    grad_scores = (weights.astype(f32) * (grad_probs - inner)).astype(bf16)
    grad_values = jnp.einsum("hgqk,qhgd->khd", weights, grad_grouped, preferred_element_type=f32)
    grad_query = jnp.einsum(
        "hgqk,khd->qhgd", grad_scores, key_rot, preferred_element_type=f32
    ) * HEAD_SIZE ** (-0.5)
    grad_key = jnp.einsum(
        "hgqk,qhgd->khd", grad_scores, grouped, preferred_element_type=f32
    ) * HEAD_SIZE ** (-0.5)
    return (grad_query.reshape(length, -1, HEAD_SIZE), grad_key, grad_values)


def body(
    tokens,
    cotangent,
    segment_ids,
    positions,
    attn_gain,
    w_query,
    key_value_weight,
    w_out,
    qk_gain,
    ffn_gain,
    w_gateup,
    w_down,
):
    parts = lax.axis_size("mp")
    sequences, length, model = tokens.shape
    width = model // parts
    offset = lax.axis_index("mp") * width
    rows, kv_heads = key_value_weight.shape[:2]
    ff = w_gateup.shape[2]
    cols = w_query.shape[1]
    kv_cols = kv_heads * 2 * HEAD_SIZE
    gain_first = attn_gain.astype(f32)
    gain_second = ffn_gain.astype(f32)
    first_part = lax.dynamic_slice_in_dim(gain_first, offset, width)
    second_part = lax.dynamic_slice_in_dim(gain_second, offset, width)
    query_gain = qk_gain[0].astype(f32)
    key_gain = qk_gain[1].astype(f32)

    attn_rows = gather_rows(
        jnp.concatenate([w_query, key_value_weight.reshape(rows, kv_cols), w_out.T], axis=1)
    )
    gateup_rows = gather_rows(w_gateup.reshape(rows, 2 * ff))
    down_rows = gather_rows(w_down.T)

    chunks = CHUNKS if sequences % CHUNKS == 0 else 1
    each = sequences // chunks
    count = each * length
    run = range(chunks)

    def cut(value, i):
        return value[i * each : (i + 1) * each]

    def flat(value, i):
        return cut(value, i).reshape((count,) + value.shape[2:])

    grad_own = [flat(cotangent, i) for i in run]
    grad_whole = [whole(grad_own[i]) for i in run]
    attn_rows, *grad_whole = after(attn_rows, *grad_whole)
    qkv_w = attn_rows[:, : cols + kv_cols]
    out_rows = attn_rows[:, cols + kv_cols :]
    normed_first, own_unit, scale_first, own = [], [], [], []
    heads = []
    attended, kept, resid = [], [], []
    for i in run:
        block = flat(tokens, i).astype(f32)
        scale = lax.rsqrt(jnp.mean(block * block, axis=-1, keepdims=True) + epsilon)
        normed_first.append((block * scale * gain_first).astype(bf16))
        part = lax.dynamic_slice_in_dim(flat(tokens, i), offset, width, 1).astype(f32)
        own.append(part)
        own_unit.append(part * scale)
        scale_first.append(scale)
        raw = jnp.dot(normed_first[i], qkv_w, preferred_element_type=f32)
        query_raw = raw[:, :cols].reshape(count, -1, HEAD_SIZE)
        keyval_raw = raw[:, cols:].reshape(count, kv_heads, 2 * HEAD_SIZE)
        cosine, sine = rotate_table(cut(positions, i).reshape(count))
        query_normed, query_unit, query_scale = head_norm(query_raw, query_gain)
        key_normed, key_unit, key_scale = head_norm(keyval_raw[..., :HEAD_SIZE], key_gain)
        shape = (each, length, -1, HEAD_SIZE)
        query_rot = rotate(query_normed, cosine, sine).astype(bf16).reshape(shape)
        key_rot = rotate(key_normed, cosine, sine).astype(bf16).reshape(shape)
        values = keyval_raw[..., HEAD_SIZE:].astype(bf16).reshape(shape)
        scores = jax.vmap(score)(query_rot, key_rot, cut(segment_ids, i))
        if i > 0:
            scores, resid[i - 1] = after(scores, resid[i - 1])
        out, weights = jax.vmap(attend)(scores, values)
        attended.append(out.reshape(count, cols))
        kept.append((query_rot, key_rot, values, weights, out))
        heads.append((cosine, sine, query_unit, query_scale, key_unit, key_scale))
        resid.append(own[i] + branch(attended[i], out_rows))

    normed_second, unit_second, scale_second = [], [], []
    hidden, gates, mixed = [], [], []
    for i in run:
        resid_all = whole(resid[i].astype(bf16)).astype(f32)
        square = row_sum(jnp.sum(resid[i] * resid[i], axis=-1))[:, None]
        scale = lax.rsqrt(square / model + epsilon)
        scale_second.append(scale)
        normed_second.append((resid_all * scale * gain_second).astype(bf16))
        unit_second.append(resid[i] * scale)
        gate = jnp.dot(normed_second[i], gateup_rows[:, :ff], preferred_element_type=f32)
        if i + 1 < chunks:
            gate, resid[i + 1] = after(gate, resid[i + 1])
        upper = jnp.dot(normed_second[i], gateup_rows[:, ff:], preferred_element_type=f32)
        sigmoid_gate = jax.nn.sigmoid(gate)
        hidden.append((gate * sigmoid_gate * upper).astype(bf16))
        gates.append((gate, upper, sigmoid_gate))
    for i in run:
        mixed.append((resid[i] + branch(hidden[i], down_rows)).astype(bf16))

    down_total = over_tokens(grad_whole, hidden)
    grad_whole[-1], down_total = after(grad_whole[-1], down_total)
    down_sum = scatter_rows(down_total).T
    grad_gateup, grad_second = [], []
    for i in run:
        gate, upper, sigmoid_gate = gates[i]
        grad_hidden = jnp.dot(grad_whole[i], down_rows, preferred_element_type=f32)
        grad_gate = grad_hidden * upper * sigmoid_gate * (1.0 + gate * (1.0 - sigmoid_gate))
        grad_upper = grad_hidden * gate * sigmoid_gate
        grad_gateup.append(
            jnp.concatenate([grad_gate.astype(bf16), grad_upper.astype(bf16)], axis=-1)
        )
        grad_second.append(branch(grad_gateup[i], gateup_rows))
    gateup_total = over_tokens(normed_second, grad_gateup)
    grad_second[-1], gateup_total = after(grad_second[-1], gateup_total)
    gateup_sum = scatter_rows(gateup_total).reshape(rows, 2, ff)

    def slice_norm_back(grad, unit, scale, gain):
        scaled = grad * gain
        inner = row_sum(jnp.sum(unit * scaled, axis=-1))[:, None]
        return (scale * (scaled - unit * (inner / model)), jnp.sum(grad * unit, axis=0))

    grad_resid, grad_branch, second_gain = [], [], 0.0
    for i in run:
        back, gain = slice_norm_back(
            grad_second[i], unit_second[i], scale_second[i], second_part
        )
        second_gain = second_gain + gain
        grad_resid.append(back + grad_own[i].astype(f32))
        grad_branch.append(whole(grad_resid[i].astype(bf16)))
    out_total = over_tokens(grad_branch, attended)
    grad_branch[-1], out_total = after(grad_branch[-1], out_total)
    out_sum = scatter_rows(out_total).T

    grad_qkv, grad_input = [], []
    first_gain = pair_gain = 0.0
    for i in run:
        cosine, sine, query_unit, query_scale, key_unit, key_scale = heads[i]
        grad_attended = jnp.dot(
            grad_branch[i], out_rows, preferred_element_type=f32
        ).astype(bf16)
        grads = jax.vmap(attend_back)(*kept[i], grad_attended.reshape(each, length, cols))
        grad_query, grad_key, grad_values = (
            value.reshape(count, -1, HEAD_SIZE) for value in grads
        )
        query_raw_grad, query_gain_grad = head_norm_back(
            rotate(grad_query, cosine, -sine), query_unit, query_scale, query_gain
        )
        key_raw_grad, key_gain_grad = head_norm_back(
            rotate(grad_key, cosine, -sine), key_unit, key_scale, key_gain
        )
        keyval_raw_grad = jnp.concatenate([key_raw_grad, grad_values], axis=-1)
        grad_qkv.append(
            jnp.concatenate(
                [
                    query_raw_grad.reshape(count, -1).astype(bf16),
                    keyval_raw_grad.reshape(count, -1).astype(bf16),
                ],
                axis=-1,
            )
        )
        grad_first = branch(grad_qkv[i], qkv_w)
        back, gain = slice_norm_back(grad_first, own_unit[i], scale_first[i], first_part)
        first_gain = first_gain + gain
        pair_gain = pair_gain + jnp.stack([query_gain_grad, key_gain_grad])
        grad_input.append(back + grad_resid[i])
    qkv_sum = scatter_rows(over_tokens(normed_first, grad_qkv))

    gains = jnp.zeros((2 * model,), f32)
    gains = lax.dynamic_update_slice_in_dim(gains, first_gain, offset, 0)
    gains = lax.dynamic_update_slice_in_dim(gains, second_gain, model + offset, 0)
    gains = lax.psum(jnp.concatenate([gains, pair_gain.reshape(-1)]), ("dp", "mp"))

    def joined(pieces):
        return jnp.concatenate(pieces, axis=0).reshape(sequences, length, width)

    return (
        joined(mixed),
        joined(grad_input),
        gains[:model],
        qkv_sum[:, :cols],
        qkv_sum[:, cols:].reshape(rows, kv_heads, 2 * HEAD_SIZE),
        out_sum,
        gains[2 * model :].reshape(2, HEAD_SIZE),
        gains[model : 2 * model],
        gateup_sum,
        down_sum,
    )


def solution(mesh):
    placed = (
        P("dp", None, None),
        P("dp", None, "mp"),
        P("dp", None),
        P("dp", None),
        P(),
        P("dp", "mp"),
        P("dp", "mp", None),
        P("mp", "dp"),
        P(),
        P(),
        P("dp", None, "mp"),
        P("mp", "dp"),
    )
    return jax.shard_map(
        body,
        mesh=mesh,
        in_specs=placed,
        out_specs=(
            P("dp", None, "mp"),
            P("dp", None, "mp"),
            P(),
            P("dp", "mp"),
            P("dp", "mp", None),
            P("mp", "dp"),
            P(),
            P(),
            P("dp", None, "mp"),
            P("mp", "dp"),
        ),
        check_vma=False,
    )
```

```python
import jax
import jax.numpy as jnp
from jax import lax
from jax.sharding import PartitionSpec as P

HEAD_SIZE = 64
CHUNKS = 2

epsilon = 1e-05
rope_base = 1000000.0
f32 = jnp.float32
bf16 = jnp.bfloat16


def rotate_table(place):
    half = HEAD_SIZE // 2
    frequency = rope_base ** (-(jnp.arange(half, dtype=f32) * 2.0 / HEAD_SIZE))
    angle = place.astype(f32)[:, None] * frequency[None, :]
    return (jnp.cos(angle)[:, None, :], jnp.sin(angle)[:, None, :])


def rotate(value, cosine, sine):
    half = HEAD_SIZE // 2
    first, second = (value[..., :half], value[..., half:])
    return jnp.concatenate(
        [first * cosine - second * sine, second * cosine + first * sine], axis=-1
    )


def head_norm(value, gain):
    scale = lax.rsqrt(jnp.mean(value * value, axis=-1, keepdims=True) + epsilon)
    unit = value * scale
    return (unit * gain, unit, scale)


def head_norm_back(grad, unit, scale, gain):
    scaled = grad * gain
    inner = jnp.mean(unit * scaled, axis=-1, keepdims=True)
    return (scale * (scaled - unit * inner), jnp.sum(grad * unit, axis=(0, 1)))


def gather_rows(part):
    return lax.all_gather(part, "dp", axis=0, tiled=True)


def scatter_rows(total):
    return lax.psum_scatter(total, "dp", scatter_dimension=0, tiled=True).astype(f32)


def after(value, *earlier):
    return lax.optimization_barrier((value,) + earlier)


def shift(value, step):
    parts = lax.axis_size("mp")
    return lax.ppermute(value, "mp", [((i + step) % parts, i) for i in range(parts)])


def whole(own):
    parts = lax.axis_size("mp")
    index = lax.axis_index("mp")
    pieces = [own] + [shift(own, step) for step in range(1, parts)]
    placed = []
    for spot in range(parts):
        piece = pieces[spot]
        for holder in range(1, parts):
            piece = jnp.where(index == holder, pieces[(spot - holder) % parts], piece)
        placed.append(piece)
    return jnp.concatenate(placed, axis=1)


def row_sum(value):
    parts = lax.axis_size("mp")
    total = value
    for step in range(1, parts):
        total = total + shift(value, step)
    return total


def total_of(value, axis):
    count = lax.axis_size(axis)
    if count & (count - 1):
        return lax.psum(value, axis)
    bit = 1
    while bit < count:
        value = value + lax.ppermute(value, axis, [(i, i ^ bit) for i in range(count)])
        bit *= 2
    return value


def branch(value, rows):
    parts = lax.axis_size("mp")
    index = lax.axis_index("mp")
    width = rows.shape[0] // parts

    def term(owner, kind):
        piece = lax.dynamic_slice_in_dim(rows, owner * width, width, 0)
        return lax.dot_general(
            value, piece, (((1,), (1,)), ((), ())), preferred_element_type=f32
        ).astype(kind)

    got = []
    for step in range(1, parts):
        got.append(shift(term(lax.rem(index + parts - step, parts), bf16), step))
    total = term(index, f32)
    for piece in got:
        total = total + piece.astype(f32)
    return total


def over_tokens(left, right):
    left = jnp.concatenate(left, axis=0)
    right = jnp.concatenate(right, axis=0)
    return lax.dot_general(
        left, right, (((0,), (0,)), ((), ())), preferred_element_type=f32
    ).astype(bf16)


def score(query_rot, key_rot, segment):
    length, kv_heads = (key_rot.shape[0], key_rot.shape[1])
    order = jnp.arange(length)
    mask = (segment[:, None] == segment[None, :]) & (order[None, :] <= order[:, None])
    grouped = query_rot.reshape(length, kv_heads, -1, HEAD_SIZE)
    scores = jnp.einsum(
        "qhgd,khd->hgqk", grouped, key_rot, preferred_element_type=f32
    ) * HEAD_SIZE ** (-0.5)
    return jnp.where(mask, scores, -1e30)


def attend(scores, values):
    length = values.shape[0]
    top = jnp.max(scores, axis=-1, keepdims=True)
    expo = jnp.exp(scores - top)
    total = jnp.sum(expo, axis=-1, keepdims=True)
    weights = (expo / total).astype(bf16)
    attended = jnp.einsum("hgqk,khd->qhgd", weights, values, preferred_element_type=f32)
    return (attended.reshape(length, -1).astype(bf16), weights)


def attend_back(query_rot, key_rot, values, weights, attended, grad_out):
    length, kv_heads = (key_rot.shape[0], key_rot.shape[1])
    shape = (length, kv_heads, -1, HEAD_SIZE)
    grouped = query_rot.reshape(shape)
    grad_grouped = grad_out.reshape(shape)
    inner = jnp.sum(attended.reshape(shape).astype(f32) * grad_grouped.astype(f32), axis=-1)
    inner = inner.transpose(1, 2, 0)[..., None]
    grad_probs = jnp.einsum("qhgd,khd->hgqk", grad_grouped, values, preferred_element_type=f32)
    grad_scores = (weights.astype(f32) * (grad_probs - inner)).astype(bf16)
    grad_values = jnp.einsum("hgqk,qhgd->khd", weights, grad_grouped, preferred_element_type=f32)
    grad_query = jnp.einsum(
        "hgqk,khd->qhgd", grad_scores, key_rot, preferred_element_type=f32
    ) * HEAD_SIZE ** (-0.5)
    grad_key = jnp.einsum(
        "hgqk,qhgd->khd", grad_scores, grouped, preferred_element_type=f32
    ) * HEAD_SIZE ** (-0.5)
    return (grad_query.reshape(length, -1, HEAD_SIZE), grad_key, grad_values)


def body(
    tokens,
    cotangent,
    segment_ids,
    positions,
    attn_gain,
    w_query,
    key_value_weight,
    w_out,
    qk_gain,
    ffn_gain,
    w_gateup,
    w_down,
):
    parts = lax.axis_size("mp")
    sequences, length, model = tokens.shape
    width = model // parts
    offset = lax.axis_index("mp") * width
    rows, kv_heads = key_value_weight.shape[:2]
    ff = w_gateup.shape[2]
    cols = w_query.shape[1]
    kv_cols = kv_heads * 2 * HEAD_SIZE
    gain_first = attn_gain.astype(f32)
    gain_second = ffn_gain.astype(f32)
    first_part = lax.dynamic_slice_in_dim(gain_first, offset, width)
    second_part = lax.dynamic_slice_in_dim(gain_second, offset, width)
    query_gain = qk_gain[0].astype(f32)
    key_gain = qk_gain[1].astype(f32)

    attn_rows = gather_rows(
        jnp.concatenate([w_query, key_value_weight.reshape(rows, kv_cols), w_out.T], axis=1)
    )
    gateup_rows = gather_rows(w_gateup.reshape(rows, 2 * ff))
    down_rows = gather_rows(w_down.T)

    chunks = CHUNKS if sequences % CHUNKS == 0 else 1
    each = sequences // chunks
    count = each * length
    run = range(chunks)

    def cut(value, i):
        return value[i * each : (i + 1) * each]

    def flat(value, i):
        return cut(value, i).reshape((count,) + value.shape[2:])

    grad_own = [flat(cotangent, i) for i in run]
    grad_whole = [whole(grad_own[i]) for i in run]
    attn_rows, *grad_whole = after(attn_rows, *grad_whole)
    qkv_w = attn_rows[:, : cols + kv_cols]
    out_rows = attn_rows[:, cols + kv_cols :]
    normed_first, own_unit, scale_first, own = [], [], [], []
    heads = []
    attended, kept, resid = [], [], []
    for i in run:
        block = flat(tokens, i).astype(f32)
        scale = lax.rsqrt(jnp.mean(block * block, axis=-1, keepdims=True) + epsilon)
        normed_first.append((block * scale * gain_first).astype(bf16))
        part = lax.dynamic_slice_in_dim(flat(tokens, i), offset, width, 1).astype(f32)
        own.append(part)
        own_unit.append(part * scale)
        scale_first.append(scale)
        raw = jnp.dot(normed_first[i], qkv_w, preferred_element_type=f32)
        query_raw = raw[:, :cols].reshape(count, -1, HEAD_SIZE)
        keyval_raw = raw[:, cols:].reshape(count, kv_heads, 2 * HEAD_SIZE)
        cosine, sine = rotate_table(cut(positions, i).reshape(count))
        query_normed, query_unit, query_scale = head_norm(query_raw, query_gain)
        key_normed, key_unit, key_scale = head_norm(keyval_raw[..., :HEAD_SIZE], key_gain)
        shape = (each, length, -1, HEAD_SIZE)
        query_rot = rotate(query_normed, cosine, sine).astype(bf16).reshape(shape)
        key_rot = rotate(key_normed, cosine, sine).astype(bf16).reshape(shape)
        values = keyval_raw[..., HEAD_SIZE:].astype(bf16).reshape(shape)
        scores = jax.vmap(score)(query_rot, key_rot, cut(segment_ids, i))
        if i > 0:
            scores, resid[i - 1] = after(scores, resid[i - 1])
        out, weights = jax.vmap(attend)(scores, values)
        attended.append(out.reshape(count, cols))
        kept.append((query_rot, key_rot, values, weights, out))
        heads.append((cosine, sine, query_unit, query_scale, key_unit, key_scale))
        resid.append(own[i] + branch(attended[i], out_rows))

    normed_second, unit_second, scale_second = [], [], []
    hidden, gates, mixed = [], [], []
    for i in run:
        resid_all = whole(resid[i].astype(bf16)).astype(f32)
        square = row_sum(jnp.sum(resid[i] * resid[i], axis=-1))[:, None]
        scale = lax.rsqrt(square / model + epsilon)
        scale_second.append(scale)
        normed_second.append((resid_all * scale * gain_second).astype(bf16))
        unit_second.append(resid[i] * scale)
        gate = jnp.dot(normed_second[i], gateup_rows[:, :ff], preferred_element_type=f32)
        if i + 1 < chunks:
            gate, resid[i + 1] = after(gate, resid[i + 1])
        upper = jnp.dot(normed_second[i], gateup_rows[:, ff:], preferred_element_type=f32)
        sigmoid_gate = jax.nn.sigmoid(gate)
        hidden.append((gate * sigmoid_gate * upper).astype(bf16))
        gates.append((gate, upper, sigmoid_gate))
    for i in run:
        mixed.append((resid[i] + branch(hidden[i], down_rows)).astype(bf16))

    down_total = over_tokens(grad_whole, hidden)
    grad_whole[-1], down_total = after(grad_whole[-1], down_total)
    down_sum = scatter_rows(down_total)
    grad_gateup, grad_second = [], []
    for i in run:
        gate, upper, sigmoid_gate = gates[i]
        grad_hidden = jnp.dot(grad_whole[i], down_rows, preferred_element_type=f32)
        grad_gate = grad_hidden * upper * sigmoid_gate * (1.0 + gate * (1.0 - sigmoid_gate))
        grad_upper = grad_hidden * gate * sigmoid_gate
        grad_gateup.append(
            jnp.concatenate([grad_gate.astype(bf16), grad_upper.astype(bf16)], axis=-1)
        )
        grad_second.append(branch(grad_gateup[i], gateup_rows))
    gateup_total = over_tokens(normed_second, grad_gateup)
    grad_second[-1], gateup_total, *mixed = after(grad_second[-1], gateup_total, *mixed)
    gateup_total, down_sum = after(gateup_total, down_sum)
    gateup_sum = scatter_rows(gateup_total)

    def slice_norm_back(grad, unit, scale, gain):
        scaled = grad * gain
        inner = row_sum(jnp.sum(unit * scaled, axis=-1))[:, None]
        return (scale * (scaled - unit * (inner / model)), jnp.sum(grad * unit, axis=0))

    grad_resid, grad_branch, second_gain = [], [], 0.0
    for i in run:
        back, gain = slice_norm_back(
            grad_second[i], unit_second[i], scale_second[i], second_part
        )
        second_gain = second_gain + gain
        grad_resid.append(back + grad_own[i].astype(f32))
        grad_branch.append(whole(grad_resid[i].astype(bf16)))
    out_total = over_tokens(grad_branch, attended)
    grad_branch[-1], out_total = after(grad_branch[-1], out_total)

    grad_qkv, grad_input = [], []
    first_gain = pair_gain = 0.0
    for i in run:
        cosine, sine, query_unit, query_scale, key_unit, key_scale = heads[i]
        grad_attended = jnp.dot(
            grad_branch[i], out_rows, preferred_element_type=f32
        ).astype(bf16)
        grads = jax.vmap(attend_back)(*kept[i], grad_attended.reshape(each, length, cols))
        grad_query, grad_key, grad_values = (
            value.reshape(count, -1, HEAD_SIZE) for value in grads
        )
        query_raw_grad, query_gain_grad = head_norm_back(
            rotate(grad_query, cosine, -sine), query_unit, query_scale, query_gain
        )
        key_raw_grad, key_gain_grad = head_norm_back(
            rotate(grad_key, cosine, -sine), key_unit, key_scale, key_gain
        )
        keyval_raw_grad = jnp.concatenate([key_raw_grad, grad_values], axis=-1)
        grad_qkv.append(
            jnp.concatenate(
                [
                    query_raw_grad.reshape(count, -1).astype(bf16),
                    keyval_raw_grad.reshape(count, -1).astype(bf16),
                ],
                axis=-1,
            )
        )
        grad_first = branch(grad_qkv[i], qkv_w)
        back, gain = slice_norm_back(grad_first, own_unit[i], scale_first[i], first_part)
        first_gain = first_gain + gain
        pair_gain = pair_gain + jnp.stack([query_gain_grad, key_gain_grad])
        grad_input.append(back + grad_resid[i])
    attn_total = jnp.concatenate([over_tokens(normed_first, grad_qkv), out_total], axis=1)
    attn_total, gateup_sum = after(attn_total, gateup_sum)
    attn_sum = scatter_rows(attn_total)
    qkv_sum, out_sum = attn_sum[:, : cols + kv_cols], attn_sum[:, cols + kv_cols :].T

    gains = jnp.zeros((2 * model,), f32)
    gains = lax.dynamic_update_slice_in_dim(gains, first_gain, offset, 0)
    gains = lax.dynamic_update_slice_in_dim(gains, second_gain, model + offset, 0)
    gains = total_of(total_of(jnp.concatenate([gains, pair_gain.reshape(-1)]), "mp"), "dp")

    def joined(pieces):
        return jnp.concatenate(pieces, axis=0).reshape(sequences, length, width)

    return (
        joined(mixed),
        joined(grad_input),
        gains[:model],
        qkv_sum[:, :cols],
        qkv_sum[:, cols:].reshape(rows, kv_heads, 2 * HEAD_SIZE),
        out_sum,
        gains[2 * model :].reshape(2, HEAD_SIZE),
        gains[model : 2 * model],
        gateup_sum.reshape(rows, 2, ff),
        down_sum.T,
    )


def solution(mesh):
    placed = (
        P("dp", None, None),
        P("dp", None, "mp"),
        P("dp", None),
        P("dp", None),
        P(),
        P("dp", "mp"),
        P("dp", "mp", None),
        P("mp", "dp"),
        P(),
        P(),
        P("dp", None, "mp"),
        P("mp", "dp"),
    )
    return jax.shard_map(
        body,
        mesh=mesh,
        in_specs=placed,
        out_specs=(
            P("dp", None, "mp"),
            P("dp", None, "mp"),
            P(),
            P("dp", "mp"),
            P("dp", "mp", None),
            P("mp", "dp"),
            P(),
            P(),
            P("dp", None, "mp"),
            P("mp", "dp"),
        ),
        check_vma=False,
    )
```
